32 devices in a mesh: dp: 4 (over y, x), seq: 4 (over z), qblk: 2 (over core).
Axes of the slice: x: 2, y: 2, z: 4, core: 2. Of those that a mesh axis runs over, the one named last changes fastest.
Arguments:
- tokens: bfloat16 [8, 2048, 1024], P('dp', ('seq', 'qblk')), may hold values from -6 to 6
- cotangent: bfloat16 [8, 2048, 1024], P('dp', ('seq', 'qblk')), may hold values from -6 to 6
- w_qkv: float32 [1024, 3072], P(('dp', 'seq'), 'qblk'), may hold values from -0.1875 to 0.1875
- w_out: float32 [1024, 1024], P(('dp', 'seq'), 'qblk'), may hold values from -6 to 6
- w_in: float32 [1024, 5248], P(('dp', 'seq'), 'qblk'), may hold values from -0.1875 to 0.1875
- w_ffn: float32 [1024, 2624], P(('dp', 'seq'), 'qblk'), may hold values from -0.125 to 0.125
- gains: float32 [2, 1024], P(None, ('dp', 'seq', 'qblk')), may hold values from 0.5 to 1.5
- first_qkv: float32 [1024, 3072], P(('dp', 'seq'), 'qblk'), may hold values from -80 to 80
- second_qkv: float32 [1024, 3072], P(('dp', 'seq'), 'qblk'), may hold values from 16.384 to 65.536
- first_out: float32 [1024, 1024], P(('dp', 'seq'), 'qblk'), may hold values from -6 to 6
- second_out: float32 [1024, 1024], P(('dp', 'seq'), 'qblk'), may hold values from 0.024 to 0.096
- first_in: float32 [1024, 5248], P(('dp', 'seq'), 'qblk'), may hold values from -32 to 32
- second_in: float32 [1024, 5248], P(('dp', 'seq'), 'qblk'), may hold values from 2.62144 to 10.48576
- first_ffn: float32 [1024, 2624], P(('dp', 'seq'), 'qblk'), may hold values from -56 to 56
- second_ffn: float32 [1024, 2624], P(('dp', 'seq'), 'qblk'), may hold values from 6.88128 to 27.8528
- first_gain: float32 [2, 1024], P(None, ('dp', 'seq', 'qblk')), may hold values from -112 to 112
- second_gain: float32 [2, 1024], P(None, ('dp', 'seq', 'qblk')), may hold values from 27.8528 to 111.4112
Outputs:
- block_out: bfloat16 [8, 2048, 1024], P('dp', ('seq', 'qblk'))
- grad_input: float32 [8, 2048, 1024], P('dp', ('seq', 'qblk'))
- first_qkv_new: float32 [1024, 3072], P(('dp', 'seq'), 'qblk')
- second_qkv_new: float32 [1024, 3072], P(('dp', 'seq'), 'qblk')
- w_qkv_new: float32 [1024, 3072], P(('dp', 'seq'), 'qblk')
- first_out_new: float32 [1024, 1024], P(('dp', 'seq'), 'qblk')
- second_out_new: float32 [1024, 1024], P(('dp', 'seq'), 'qblk')
- w_out_new: float32 [1024, 1024], P(('dp', 'seq'), 'qblk')
- first_in_new: float32 [1024, 5248], P(('dp', 'seq'), 'qblk')
- second_in_new: float32 [1024, 5248], P(('dp', 'seq'), 'qblk')
- w_in_new: float32 [1024, 5248], P(('dp', 'seq'), 'qblk')
- first_ffn_new: float32 [1024, 2624], P(('dp', 'seq'), 'qblk')
- second_ffn_new: float32 [1024, 2624], P(('dp', 'seq'), 'qblk')
- w_ffn_new: float32 [1024, 2624], P(('dp', 'seq'), 'qblk')
- first_gain_new: float32 [2, 1024], P(None, ('dp', 'seq', 'qblk'))
- second_gain_new: float32 [2, 1024], P(None, ('dp', 'seq', 'qblk'))
- gains_new: float32 [2, 1024], P(None, ('dp', 'seq', 'qblk'))
The draws below stay inside these ranges and needn't reach their ends.
All inputs are finite; a program needn't handle non-finite values.
Results may differ from the reference program's by a relative error of at most 0.02.
Values may be sent and summed in bfloat16 or wider, within the bound.
A program may use at most 320 MiB of HBM per device.

```python
import math
import jax
import jax.numpy as jnp
from jax import lax

D = 1024
H = 16
HD = 64
FF = 2624
SEQS = 2
LENGTH = 2048
STEP = 10
OUT_FAN = 1
TOKENS = 16384
N_DP = 4


def raised(drawn, stream_key, source, target, parts, factor):
    owner, partner = [(jnp.arange(drawn.shape[dim]) // (drawn.shape[dim] // parts)).reshape([-1 if axis == dim else 1 for axis in range(drawn.ndim)]) for dim in (source, target)]
    chosen = jax.random.permutation(stream_key, parts)[partner]
    strong = (owner == chosen) | (owner == (partner + parts // 2) % parts)
    return jnp.where(strong, factor * drawn, drawn)


def shard_levels(stream_key, dims, shards, least, largest):
    gain = 1.0
    for axis_at, shards_of in shards:
        draws = jax.random.uniform(jax.random.fold_in(jax.random.fold_in(stream_key, 6), axis_at), (shards_of,), jnp.float32, least / len(shards), largest / len(shards))
        gain = gain * jnp.repeat(jnp.exp(draws), dims[axis_at] // shards_of).reshape((-1,) + (1,) * (len(dims) - 1 - axis_at))
    return gain


def scatter_about(key, dims, deviation, reach, split=(), kind=jnp.bfloat16):
    gain = shard_levels(key, dims, split, -0.22, 0.18) if split else 1.0
    array = jax.random.normal(key, dims, jnp.float32) * deviation * gain
    return jnp.minimum(jnp.maximum(array, -reach), reach).astype(kind)


def heavy_noise(rng, dims, scale, most, split, heavy, kind=jnp.bfloat16):
    array = scale * jax.random.normal(rng, dims, jnp.float32)
    if split:
        array = array * shard_levels(rng, dims, split, -0.22, 0.18)
    return jnp.clip(raised(array, jax.random.fold_in(rng, 3), *heavy), -most, most).astype(kind)


def setup_inputs(seed: int = 0) -> dict:
    splits = jax.random.split(jax.random.key(seed), 18)
    tokens = scatter_about(splits[0], (SEQS * N_DP, LENGTH, D), 1.0, 6.0, ((0, 4), (1, 8)))
    cotangent = heavy_noise(splits[1], (SEQS * N_DP, LENGTH, D), 1.0, 6.0, ((0, 4), (1, 8)), (1, 2, 8, 2.0))
    w_qkv = scatter_about(splits[2], (D, 3 * D), D ** -0.5, 0.1875, ((0, 16), (1, 2)), jnp.float32)
    w_out = scatter_about(splits[3], (D, D), OUT_FAN ** -0.5, 6.0, ((0, 16), (1, 2)), jnp.float32)
    w_in = scatter_about(splits[4], (D, 2 * FF), D ** -0.5, 0.1875, ((0, 16), (1, 2)), jnp.float32)
    w_ffn = scatter_about(splits[5], (D, FF), FF ** -0.5, 0.125, ((0, 16), (1, 2)), jnp.float32)
    gains = jnp.clip(1.0 + 0.1 * jax.random.normal(splits[6], (2, D), jnp.float32), 0.5, 1.5)
    first_qkv = scatter_about(splits[7], (D, 3 * D), (0.11 * TOKENS ** 0.5), 80.0, ((0, 16), (1, 2)), jnp.float32)
    second_qkv = jnp.clip(jnp.exp(math.log(65.536) - 1.3862944 * jax.random.uniform(splits[8], (D, 3 * D), jnp.float32) ** shard_levels(splits[8], (D, 3 * D), ((0, 16), (1, 2)), -0.2, 0.2)), 16.384, 65.536)
    first_out = scatter_about(splits[9], (D, D), (0.11 * (3 * TOKENS // LENGTH) ** 0.5), 6.0, ((0, 16), (1, 2)), jnp.float32)
    second_out = jnp.clip(jnp.exp(math.log(0.096) - 1.3862944 * jax.random.uniform(splits[10], (D, D), jnp.float32) ** shard_levels(splits[10], (D, D), ((0, 16), (1, 2)), -0.2, 0.2)), 0.024, 0.096)
    first_in = scatter_about(splits[11], (D, 2 * FF), (0.045 * TOKENS ** 0.5), 32.0, ((0, 16), (1, 2)), jnp.float32)
    second_in = jnp.clip(jnp.exp(math.log(10.48576) - 1.3862944 * jax.random.uniform(splits[12], (D, 2 * FF), jnp.float32) ** shard_levels(splits[12], (D, 2 * FF), ((0, 16), (1, 2)), -0.2, 0.2)), 2.62144, 10.48576)
    first_ffn = scatter_about(splits[13], (D, FF), (0.07 * TOKENS ** 0.5), 56.0, ((0, 16), (1, 2)), jnp.float32)
    second_ffn = jnp.clip(jnp.exp(math.log(27.8528) - 1.39812884 * jax.random.uniform(splits[14], (D, FF), jnp.float32) ** shard_levels(splits[14], (D, FF), ((0, 16), (1, 2)), -0.2, 0.2)), 6.88128, 27.8528)
    first_gain = scatter_about(splits[15], (2, D), (0.14 * TOKENS ** 0.5), 112.0, ((1, 32),), jnp.float32)
    second_gain = jnp.clip(jnp.exp(math.log(111.4112) - 1.3862944 * jax.random.uniform(splits[16], (2, D), jnp.float32) ** shard_levels(splits[16], (2, D), ((1, 32),), -0.2, 0.2)), 27.8528, 111.4112)
    return dict(tokens=tokens, cotangent=cotangent, w_qkv=w_qkv, w_out=w_out, w_in=w_in, w_ffn=w_ffn, gains=gains, first_qkv=first_qkv, second_qkv=second_qkv, first_out=first_out, second_out=second_out, first_in=first_in, second_in=second_in, first_ffn=first_ffn, second_ffn=second_ffn, first_gain=first_gain, second_gain=second_gain)


@jax.custom_vjp
def low(v):
    return lax.optimization_barrier(v.astype(jnp.bfloat16)).astype(jnp.float32)

@jax.custom_vjp
def low_back(v):
    return v

def low_keep(v):
    return (low(v), None)

def low_pass(kept, grad):
    return (grad,)

def back_keep(v):
    return (v, None)

def back_low(kept, grad):
    return (low(grad),)
low.defvjp(low_keep, low_pass)
low_back.defvjp(back_keep, back_low)
EPS_NORM = 1e-05
ROPE_BASE = 160000.0
BETA_ONE = 0.9
BETA_TWO = 0.999
ADAM_EPS = 1e-08
WEIGHT_DECAY = 0.01
LR_FACTOR = 3.0
LR_GAIN = 1.0

def matmul(left, right):
    return jnp.dot(left, right, precision=lax.Precision.HIGHEST, preferred_element_type=jnp.float32)

def rotary(values, places):
    half_dim = HD // 2
    inv_freq = ROPE_BASE ** (-2.0 * jnp.arange(half_dim, dtype=jnp.float32) / HD)
    angles = places[:, None] * inv_freq[None, :]
    cos_part = jnp.cos(angles)[:, None, :]
    sin_part = jnp.sin(angles)[:, None, :]
    lower_half = values[..., :half_dim]
    upper_half = values[..., half_dim:]
    return jnp.concatenate([lower_half * cos_part - upper_half * sin_part, upper_half * cos_part + lower_half * sin_part], axis=-1)

def norm_apply(values, gain_row):
    row_mean = lax.optimization_barrier(jnp.mean(values, axis=-1, keepdims=True))
    centered = values - row_mean
    row_var = lax.optimization_barrier(jnp.mean(centered * centered, axis=-1, keepdims=True))
    return centered * lax.rsqrt(row_var + EPS_NORM) * gain_row

def gated(gate_part, up_part):
    return jax.nn.gelu(gate_part, approximate=False) * up_part

def one_sequence(seq_rows, low_qkv, low_out, low_in, low_ffn, low_gain):
    positions = jnp.arange(LENGTH, dtype=jnp.float32)
    attn_in = low(norm_apply(seq_rows, low_gain[0]))
    proj_qkv = low_back(low(matmul(attn_in, low_qkv))).reshape(LENGTH, 3, H, HD)
    q_rot = low(rotary(proj_qkv[:, 0], positions))
    k_rot = low(rotary(proj_qkv[:, 1], positions))
    v_rows = proj_qkv[:, 2]
    scores = jnp.einsum('qhd,khd->hqk', q_rot, k_rot, precision=lax.Precision.HIGHEST) * HD ** (-0.5)
    scores = low_back(scores)
    row_max = lax.optimization_barrier(jnp.max(scores, axis=-1, keepdims=True))
    exp_scores = jnp.exp(scores - row_max)
    probs = low(exp_scores / lax.optimization_barrier(jnp.sum(exp_scores, axis=-1, keepdims=True)))
    attn = jnp.einsum('hqk,khd->qhd', probs, v_rows, precision=lax.Precision.HIGHEST)
    attn = low_back(low(attn)).reshape(LENGTH, D)
    resid_mid = seq_rows + low_back(matmul(attn, low_out))
    ffn_in = low(norm_apply(resid_mid, low_gain[1]))
    gate_up = low_back(matmul(ffn_in, low_in))
    hidden = low(gated(gate_up[:, :FF], gate_up[:, FF:]))
    return resid_mid + low_back(matmul(hidden, low_ffn.T))

def adam_step(weight, grad_sum, moment, second, learn_rate, weight_decay):
    moment_new = BETA_ONE * moment + (1.0 - BETA_ONE) * grad_sum
    second_new = BETA_TWO * second + (1.0 - BETA_TWO) * grad_sum * grad_sum
    update = moment_new / (1.0 - BETA_ONE ** STEP) / (jnp.sqrt(second_new / (1.0 - BETA_TWO ** STEP)) + ADAM_EPS)
    return (moment_new, second_new, weight - learn_rate * (update + weight_decay * weight))

def reference(tokens, cotangent, w_qkv, w_out, w_in, w_ffn, gains, first_qkv, second_qkv, first_out, second_out, first_in, second_in, first_ffn, second_ffn, first_gain, second_gain):

    def forward(resid_all, weight_qkv, weight_out, weight_in, weight_ffn, weight_gain):
        low_qkv = low(weight_qkv)
        low_out = low(weight_out)
        low_in = low(weight_in)
        low_ffn = low(weight_ffn)
        low_gain = low(weight_gain)
        per_sequence = jax.checkpoint(one_sequence)
        return lax.map(lambda seq_rows: per_sequence(seq_rows, low_qkv, low_out, low_in, low_ffn, low_gain), resid_all)
    block, pullback = jax.vjp(forward, tokens.astype(jnp.float32), w_qkv, w_out, w_in, w_ffn, gains)
    grad_x, grad_qkv, grad_out, grad_in, grad_ffn, grad_gain = pullback(cotangent.astype(jnp.float32))
    new_qkv = adam_step(w_qkv, grad_qkv, first_qkv, second_qkv, LR_FACTOR * D ** (-0.5), WEIGHT_DECAY)
    new_out = adam_step(w_out, grad_out, first_out, second_out, LR_FACTOR * OUT_FAN ** (-0.5), WEIGHT_DECAY)
    new_in = adam_step(w_in, grad_in, first_in, second_in, LR_FACTOR * D ** (-0.5), WEIGHT_DECAY)
    new_ffn = adam_step(w_ffn, grad_ffn, first_ffn, second_ffn, LR_FACTOR * FF ** (-0.5), WEIGHT_DECAY)
    new_gain = adam_step(gains, grad_gain, first_gain, second_gain, LR_GAIN, 0.0)
    return (block.astype(jnp.bfloat16), grad_x, new_qkv[0], new_qkv[1], new_qkv[2], new_out[0], new_out[1], new_out[2], new_in[0], new_in[1], new_in[2], new_ffn[0], new_ffn[1], new_ffn[2], new_gain[0], new_gain[1], new_gain[2])
```

```python
import jax
import jax.numpy as jnp
from jax import lax
from jax.experimental import pallas as pl
from jax.experimental.pallas import tpu as pltpu
from jax.sharding import PartitionSpec as P

D = 1024
H = 16
HD = 64
FF = 2624
STEP = 10
OUT_FAN = 1


EPS_NORM = 1e-05
ROPE_BASE = 160000.0
BETA_ONE = 0.9
BETA_TWO = 0.999
ADAM_EPS = 1e-08
WEIGHT_DECAY = 0.01
LR_FACTOR = 3.0
LR_GAIN = 1.0


def rotate(rows, cos_part, sin_part):
    half = HD // 2
    low_half = rows[:half]
    high_half = rows[half:]
    return jnp.concatenate(
        [
            low_half * cos_part - high_half * sin_part,
            high_half * cos_part + low_half * sin_part,
        ],
        axis=0,
    )


def mm(left, right):
    return jnp.dot(left, right, preferred_element_type=jnp.float32)


def attend_kernel(qkv_ref, cos_ref, sin_ref, out_ref, lse_ref, q_s, k_s, v_s):
    parts, _, _, _, cols = qkv_ref.shape
    for z in range(parts):
        at = slice(z * cols, (z + 1) * cols)
        cos_part, sin_part = cos_ref[z], sin_ref[z]
        q_rot = rotate(qkv_ref[z, 0, 0].astype(jnp.float32), cos_part, sin_part)
        q_s[z] = (q_rot.astype(jnp.bfloat16).astype(jnp.float32) * HD ** (-0.5)).astype(jnp.bfloat16)
        k_rot = rotate(qkv_ref[z, 0, 1].astype(jnp.float32), cos_part, sin_part)
        k_s[at, :] = k_rot.T.astype(jnp.bfloat16)
        v_s[:, at] = qkv_ref[z, 0, 2]

    def block(z, carry):
        scores = mm(k_s[...], q_s[z])
        top = jnp.max(scores, axis=0, keepdims=True)
        exp_scores = jnp.exp(scores - top)
        total = jnp.sum(exp_scores, axis=0, keepdims=True)
        out = mm(v_s[...], exp_scores.astype(jnp.bfloat16))
        out_ref[z, 0] = (out / total).astype(jnp.bfloat16)
        lse_ref[z, 0] = top + jnp.log(total)
        return carry

    lax.fori_loop(0, parts, block, 0)


def attend_back_kernel(
    qkv_ref, cos_ref, sin_ref, out_ref, lse_ref, grad_ref, res_ref,
    q_s, q_rows, k_s, k_cols, v_rows, g_rows, dk, dv,
):
    parts, _, _, _, cols = qkv_ref.shape
    for z in range(parts):
        at = slice(z * cols, (z + 1) * cols)
        cos_part, sin_part = cos_ref[z], sin_ref[z]
        q_rot = rotate(qkv_ref[z, 0, 0].astype(jnp.float32), cos_part, sin_part)
        q_rot = q_rot.astype(jnp.bfloat16).astype(jnp.float32) * HD ** (-0.5)
        q_s[z] = q_rot.astype(jnp.bfloat16)
        q_rows[z] = q_rot.T.astype(jnp.bfloat16)
        k_rot = rotate(qkv_ref[z, 0, 1].astype(jnp.float32), cos_part, sin_part)
        k_cols[:, at] = k_rot.astype(jnp.bfloat16)
        k_s[at, :] = k_rot.T.astype(jnp.bfloat16)
        v_rows[at, :] = qkv_ref[z, 0, 2].astype(jnp.float32).T.astype(jnp.bfloat16)
        g_rows[z] = grad_ref[z, 0].astype(jnp.float32).T.astype(jnp.bfloat16)
    dk[...] = jnp.zeros_like(dk)
    dv[...] = jnp.zeros_like(dv)

    def block(z, carry):
        grad = grad_ref[z, 0]
        inner = jnp.sum(
            grad.astype(jnp.float32) * out_ref[z, 0].astype(jnp.float32), axis=0, keepdims=True
        )
        probs = jnp.exp(mm(k_s[...], q_s[z]) - lse_ref[z, 0])
        dv[...] += mm(probs.astype(jnp.bfloat16), g_rows[z])
        score_grad = (probs * (mm(v_rows[...], grad) - inner)).astype(jnp.bfloat16)
        dk[...] += mm(score_grad, q_rows[z])
        dq = mm(k_cols[...], score_grad) * HD ** (-0.5)
        res_ref[z, 0, 0] = rotate(dq, cos_ref[z], -sin_ref[z]).astype(jnp.bfloat16)
        return carry

    lax.fori_loop(0, parts, block, 0)
    for z in range(parts):
        at = slice(z * cols, (z + 1) * cols)
        dk_cols = dk[at, :].T
        res_ref[z, 0, 1] = rotate(dk_cols, cos_ref[z], -sin_ref[z]).astype(jnp.bfloat16)
        res_ref[z, 0, 2] = dv[at, :].T.astype(jnp.bfloat16)


def pair_spec(parts, *rest):
    zeros = (0,) * len(rest)
    return pl.BlockSpec((parts, 1) + rest, lambda pair: (0, pair) + zeros)


def attend(qkv, cos_tab, sin_tab):
    parts, pairs, _, _, cols = qkv.shape
    length = parts * cols
    table = pl.BlockSpec(cos_tab.shape, lambda pair: (0, 0, 0))
    return pl.pallas_call(
        attend_kernel,
        grid=(pairs,),
        in_specs=[pair_spec(parts, 3, HD, cols), table, table],
        out_specs=[pair_spec(parts, HD, cols), pair_spec(parts, 1, cols)],
        out_shape=[
            jax.ShapeDtypeStruct((parts, pairs, HD, cols), jnp.bfloat16),
            jax.ShapeDtypeStruct((parts, pairs, 1, cols), jnp.float32),
        ],
        scratch_shapes=[
            pltpu.VMEM((parts, HD, cols), jnp.bfloat16),
            pltpu.VMEM((length, HD), jnp.bfloat16),
            pltpu.VMEM((HD, length), jnp.bfloat16),
        ],
        compiler_params=pltpu.CompilerParams(vmem_limit_bytes=40 * 2**20),
        cost_estimate=pl.CostEstimate(
            flops=16 * pairs * length * length * HD,
            bytes_accessed=8 * pairs * length * HD,
            transcendentals=pairs * length * length,
        ),
        name="attend",
    )(qkv, cos_tab, sin_tab)


def attend_back(qkv, cos_tab, sin_tab, out, lse, grad):
    parts, pairs, _, _, cols = qkv.shape
    length = parts * cols
    table = pl.BlockSpec(cos_tab.shape, lambda pair: (0, 0, 0))
    return pl.pallas_call(
        attend_back_kernel,
        grid=(pairs,),
        in_specs=[
            pair_spec(parts, 3, HD, cols),
            table,
            table,
            pair_spec(parts, HD, cols),
            pair_spec(parts, 1, cols),
            pair_spec(parts, HD, cols),
        ],
        out_specs=pair_spec(parts, 3, HD, cols),
        out_shape=jax.ShapeDtypeStruct(qkv.shape, jnp.bfloat16),
        scratch_shapes=[
            pltpu.VMEM((parts, HD, cols), jnp.bfloat16),
            pltpu.VMEM((parts, cols, HD), jnp.bfloat16),
            pltpu.VMEM((length, HD), jnp.bfloat16),
            pltpu.VMEM((HD, length), jnp.bfloat16),
            pltpu.VMEM((length, HD), jnp.bfloat16),
            pltpu.VMEM((parts, cols, HD), jnp.bfloat16),
            pltpu.VMEM((length, HD), jnp.float32),
            pltpu.VMEM((length, HD), jnp.float32),
        ],
        compiler_params=pltpu.CompilerParams(vmem_limit_bytes=48 * 2**20),
        cost_estimate=pl.CostEstimate(
            flops=40 * pairs * length * length * HD,
            bytes_accessed=20 * pairs * length * HD,
            transcendentals=pairs * length * length,
        ),
        name="attend_back",
    )(qkv, cos_tab, sin_tab, out, lse, grad)


def swap(values):
    return lax.ppermute(values, "qblk", [(0, 1), (1, 0)])


def norm_fwd(values, gain_row):
    row_mean = jnp.mean(values, axis=-1, keepdims=True)
    centered = values - row_mean
    row_var = jnp.mean(centered * centered, axis=-1, keepdims=True)
    inv_std = lax.rsqrt(row_var + EPS_NORM)
    normed = centered * inv_std
    return (normed, inv_std, (normed * gain_row).astype(jnp.bfloat16))


def norm_back(upstream, normed, inv_std, gain_row):
    scaled = upstream * gain_row
    return inv_std * (
        scaled
        - jnp.mean(scaled, axis=-1, keepdims=True)
        - normed * jnp.mean(scaled * normed, axis=-1, keepdims=True)
    )


def gated(gate_part, up_part):
    return jax.nn.gelu(gate_part, approximate=False) * up_part


def adam_step(weight, grad_sum, moment, second, learn_rate, weight_decay):
    moment_new = BETA_ONE * moment + (1.0 - BETA_ONE) * grad_sum
    second_new = BETA_TWO * second + (1.0 - BETA_TWO) * grad_sum * grad_sum
    update = (
        moment_new
        / (1.0 - BETA_ONE**STEP)
        / (jnp.sqrt(second_new / (1.0 - BETA_TWO**STEP)) + ADAM_EPS)
    )
    return (moment_new, second_new, weight - learn_rate * (update + weight_decay * weight))


def on_device(
    tokens,
    cotangent,
    w_qkv,
    w_out,
    w_in,
    w_ffn,
    gains,
    first_qkv,
    second_qkv,
    first_out,
    second_out,
    first_in,
    second_in,
    first_ffn,
    second_ffn,
    first_gain,
    second_gain,
):
    n_seq = lax.axis_size("seq")
    core = lax.axis_index("qblk")
    first = core == 0
    seq_count, tok_local, width = tokens.shape
    row_count = seq_count * tok_local
    chip_tok = 2 * tok_local
    heads = H // 2
    pairs = heads * seq_count // n_seq
    both = ("dp", "seq")

    def ordered(own, other, axis):
        return jnp.where(
            first,
            jnp.concatenate([own, other], axis=axis),
            jnp.concatenate([other, own], axis=axis),
        )

    def gather(shard):
        return lax.all_gather(shard, both, axis=0, tiled=True)

    def scatter(grad):
        return lax.psum_scatter(grad, both, scatter_dimension=0, tiled=True)

    def with_other(rows):
        return jnp.concatenate([rows, swap(rows)], axis=0)

    def sum_own(part):
        other = swap(part[row_count:].astype(jnp.bfloat16))
        return part[:row_count] + other.astype(jnp.float32)

    third = w_qkv.shape[1] // 3
    low_qkv = w_qkv.astype(jnp.bfloat16)
    col_a, col_b, col_c = low_qkv[:, :third], low_qkv[:, third : 2 * third], low_qkv[:, 2 * third :]
    col_r = swap(col_b)
    full_gain = lax.all_gather(
        gains.astype(jnp.bfloat16), ("dp", "seq", "qblk"), axis=1, tiled=True
    )
    full_qkv = gather(
        jnp.where(
            first,
            jnp.concatenate([col_a, col_c, col_r], axis=1),
            jnp.concatenate([col_r, col_a, col_c], axis=1),
        )
    )
    low_out = w_out.astype(jnp.bfloat16)
    shard_out = ordered(low_out, swap(low_out), 1)
    low_in = w_in.astype(jnp.bfloat16)
    part = low_in.shape[1] // 2
    in_r = swap(jnp.where(first, low_in[:, part:], low_in[:, :part]))
    shard_gate = jnp.where(first, low_in[:, :part], in_r)
    shard_up = jnp.where(first, in_r, low_in[:, part:])
    low_ffn = w_ffn.astype(jnp.bfloat16)
    full_qkv, shard_out, shard_gate, shard_up, low_ffn = lax.optimization_barrier(
        (full_qkv, shard_out, shard_gate, shard_up, low_ffn)
    )
    full_out = gather(shard_out)
    full_gate = gather(shard_gate)
    full_up = gather(shard_up)
    full_ffn = gather(low_ffn)

    place_ids = jnp.arange(n_seq * chip_tok, dtype=jnp.int32).reshape(n_seq, 1, chip_tok)
    in_chip = place_ids % chip_tok
    positions = (
        place_ids - in_chip + (in_chip // tok_local + core) % 2 * tok_local + in_chip % tok_local
    ).astype(jnp.float32)
    half_dim = HD // 2
    inv_freq = ROPE_BASE ** (-2.0 * jnp.arange(half_dim, dtype=jnp.float32) / HD)
    angles = inv_freq[None, :, None] * positions
    cos_tab, sin_tab = jnp.cos(angles), jnp.sin(angles)

    def to_heads(cols, kinds):
        split = cols.reshape(kinds, heads, HD, 2, seq_count, tok_local)
        split = split.transpose(1, 4, 0, 2, 3, 5).reshape(n_seq, pairs, kinds, HD, chip_tok)
        return lax.all_to_all(split, "seq", split_axis=0, concat_axis=0, tiled=True)

    def from_heads(moved, kinds):
        back = lax.all_to_all(moved, "seq", split_axis=0, concat_axis=0, tiled=True)
        back = back.reshape(heads, seq_count, kinds, HD, 2, tok_local)
        return back.transpose(2, 0, 3, 4, 1, 5).reshape(kinds * heads * HD, 2 * row_count)

    gain_rows = full_gain.astype(jnp.float32)
    resid_in = tokens.astype(jnp.float32).reshape(row_count, width)
    normed_one, inv_one, attn_own = norm_fwd(resid_in, gain_rows[0])
    attn_in = with_other(attn_own)
    grad_own = cotangent.reshape(row_count, width).astype(jnp.bfloat16)
    grad_low = with_other(grad_own)
    proj = jnp.einsum("dn,td->nt", full_qkv, attn_in, preferred_element_type=jnp.float32)
    qkv = to_heads(proj.astype(jnp.bfloat16), 3)
    head_out, lse = attend(qkv, cos_tab, sin_tab)
    attn_cols = from_heads(head_out[:, :, None], 1)
    attn = ordered(attn_cols[:, :row_count], swap(attn_cols[:, row_count:]), 0)
    resid_mid = resid_in + jnp.einsum(
        "ft,fd->td", attn, full_out, preferred_element_type=jnp.float32
    )
    normed_two, inv_two, ffn_own = norm_fwd(resid_mid, gain_rows[1])
    ffn_in = with_other(ffn_own)
    gate_part = mm(ffn_in, full_gate)
    up_part = mm(ffn_in, full_up)
    hidden = gated(gate_part, up_part).astype(jnp.bfloat16)
    hidden_grad = mm(grad_low, full_ffn)
    gate_grad, up_grad = jax.vjp(gated, gate_part, up_part)[1](hidden_grad)
    gate_grad = gate_grad.astype(jnp.bfloat16)
    up_grad = up_grad.astype(jnp.bfloat16)

    def outer(left, right):
        return jnp.einsum("ta,tb->ab", left, right, preferred_element_type=jnp.float32).astype(
            jnp.bfloat16
        )

    def times_t(left, right):
        return jnp.einsum("tf,df->td", left, right, preferred_element_type=jnp.float32)

    ffn_in_grad = sum_own(times_t(gate_grad, full_gate) + times_t(up_grad, full_up))
    gain_two_grad = jnp.sum(ffn_in_grad * normed_two, axis=0)
    grad_y = cotangent.astype(jnp.float32).reshape(row_count, width)
    mid_grad = grad_y + norm_back(ffn_in_grad, normed_two, inv_two, gain_rows[1])
    mid_low = mid_grad.astype(jnp.bfloat16)
    grad_gate = outer(ffn_in, gate_grad)
    grad_up = outer(ffn_in, up_grad)
    grad_ffn = outer(grad_low, hidden)
    attn_grad = jnp.einsum("fd,td->ft", full_out, mid_low, preferred_element_type=jnp.float32)
    attn_grad = attn_grad.astype(jnp.bfloat16)
    span = heads * HD
    mine = lax.dynamic_slice_in_dim(attn_grad, core * span, span, axis=0)
    theirs = lax.dynamic_slice_in_dim(attn_grad, (1 - core) * span, span, axis=0)
    heads_grad = to_heads(jnp.concatenate([mine, swap(theirs)], axis=1), 1)
    heads_grad, grad_gate, grad_up, grad_ffn = lax.optimization_barrier(
        (heads_grad, grad_gate, grad_up, grad_ffn)
    )
    sum_gate = scatter(grad_gate)
    sum_up = scatter(grad_up)
    sum_ffn = scatter(grad_ffn).astype(jnp.float32)
    grad_out = jnp.einsum("ft,td->fd", attn, mid_low, preferred_element_type=jnp.float32)
    out_cols = w_out.shape[1]
    out_mine = lax.dynamic_slice_in_dim(grad_out, core * out_cols, out_cols, axis=1)
    out_theirs = lax.dynamic_slice_in_dim(grad_out, (1 - core) * out_cols, out_cols, axis=1)
    out_sum = out_mine + swap(out_theirs.astype(jnp.bfloat16)).astype(jnp.float32)
    sum_out = scatter(out_sum.astype(jnp.bfloat16)).astype(jnp.float32)
    block_part = times_t(hidden, full_ffn)
    block_out = (resid_mid + sum_own(block_part)).astype(jnp.bfloat16).reshape(tokens.shape)

    res = attend_back(qkv, cos_tab, sin_tab, head_out, lse, heads_grad[:, :, 0])
    qkv_grad = from_heads(res, 3)
    grad_qkv = jnp.einsum("td,nt->dn", attn_in, qkv_grad, preferred_element_type=jnp.float32)
    rows_qkv = scatter(grad_qkv.astype(jnp.bfloat16))
    in_grad = sum_own(
        jnp.einsum("nt,dn->td", qkv_grad, full_qkv, preferred_element_type=jnp.float32)
    )
    gain_one_grad = jnp.sum(in_grad * normed_one, axis=0)
    grad_x = mid_grad + norm_back(in_grad, normed_one, inv_one, gain_rows[0])
    sum_gain = lax.psum_scatter(
        jnp.stack([gain_one_grad, gain_two_grad]),
        ("dp", "seq", "qblk"),
        scatter_dimension=1,
        tiled=True,
    )
    q_sum, k_sum, v_sum = rows_qkv[:, :third], rows_qkv[:, third : 2 * third], rows_qkv[:, 2 * third :]
    qkv_r = swap(jnp.where(first, v_sum, q_sum))
    sum_qkv = jnp.concatenate(
        [jnp.where(first, q_sum, k_sum), qkv_r, jnp.where(first, k_sum, v_sum)], axis=1
    ).astype(jnp.float32)
    gate_up_r = swap(jnp.where(first, sum_up, sum_gate))
    sum_in = ordered(jnp.where(first, sum_gate, sum_up), gate_up_r, 1).astype(jnp.float32)
    new_qkv = adam_step(
        w_qkv, sum_qkv, first_qkv, second_qkv, LR_FACTOR * D ** (-0.5), WEIGHT_DECAY
    )
    new_out = adam_step(
        w_out, sum_out, first_out, second_out, LR_FACTOR * OUT_FAN ** (-0.5), WEIGHT_DECAY
    )
    new_in = adam_step(w_in, sum_in, first_in, second_in, LR_FACTOR * D ** (-0.5), WEIGHT_DECAY)
    new_ffn = adam_step(
        w_ffn, sum_ffn, first_ffn, second_ffn, LR_FACTOR * FF ** (-0.5), WEIGHT_DECAY
    )
    new_gain = adam_step(gains, sum_gain, first_gain, second_gain, LR_GAIN, 0.0)
    return (
        block_out,
        grad_x.reshape(tokens.shape),
        new_qkv[0],
        new_qkv[1],
        new_qkv[2],
        new_out[0],
        new_out[1],
        new_out[2],
        new_in[0],
        new_in[1],
        new_in[2],
        new_ffn[0],
        new_ffn[1],
        new_ffn[2],
        new_gain[0],
        new_gain[1],
        new_gain[2],
    )


def solution(mesh):
    placed = (
        P("dp", ("seq", "qblk"), None),
        P("dp", ("seq", "qblk"), None),
        P(("dp", "seq"), "qblk"),
        P(("dp", "seq"), "qblk"),
        P(("dp", "seq"), "qblk"),
        P(("dp", "seq"), "qblk"),
        P(None, ("dp", "seq", "qblk")),
        P(("dp", "seq"), "qblk"),
        P(("dp", "seq"), "qblk"),
        P(("dp", "seq"), "qblk"),
        P(("dp", "seq"), "qblk"),
        P(("dp", "seq"), "qblk"),
        P(("dp", "seq"), "qblk"),
        P(("dp", "seq"), "qblk"),
        P(("dp", "seq"), "qblk"),
        P(None, ("dp", "seq", "qblk")),
        P(None, ("dp", "seq", "qblk")),
    )
    return jax.shard_map(
        on_device,
        mesh=mesh,
        in_specs=placed,
        out_specs=(
            P("dp", ("seq", "qblk"), None),
            P("dp", ("seq", "qblk"), None),
            P(("dp", "seq"), "qblk"),
            P(("dp", "seq"), "qblk"),
            P(("dp", "seq"), "qblk"),
            P(("dp", "seq"), "qblk"),
            P(("dp", "seq"), "qblk"),
            P(("dp", "seq"), "qblk"),
            P(("dp", "seq"), "qblk"),
            P(("dp", "seq"), "qblk"),
            P(("dp", "seq"), "qblk"),
            P(("dp", "seq"), "qblk"),
            P(("dp", "seq"), "qblk"),
            P(("dp", "seq"), "qblk"),
            P(None, ("dp", "seq", "qblk")),
            P(None, ("dp", "seq", "qblk")),
            P(None, ("dp", "seq", "qblk")),
        ),
        check_vma=False,
    )
```

```python
import jax
import jax.numpy as jnp
from jax import lax
from jax.experimental import pallas as pl
from jax.experimental.pallas import tpu as pltpu
from jax.sharding import PartitionSpec as P

D = 1024
H = 16
HD = 64
FF = 2624
STEP = 10
OUT_FAN = 1


EPS_NORM = 1e-05
ROPE_BASE = 160000.0
BETA_ONE = 0.9
BETA_TWO = 0.999
ADAM_EPS = 1e-08
WEIGHT_DECAY = 0.01
LR_FACTOR = 3.0
LR_GAIN = 1.0


def rotate(rows, cos_part, sin_part):
    half = HD // 2
    low_half = rows[:half]
    high_half = rows[half:]
    return jnp.concatenate(
        [
            low_half * cos_part - high_half * sin_part,
            high_half * cos_part + low_half * sin_part,
        ],
        axis=0,
    )


def mm(left, right):
    return jnp.dot(left, right, preferred_element_type=jnp.float32)


def attend_kernel(qkv_ref, cos_ref, sin_ref, out_ref, lse_ref, q_s, k_s, v_s):
    parts, _, _, _, cols = qkv_ref.shape
    for z in range(parts):
        at = slice(z * cols, (z + 1) * cols)
        cos_part, sin_part = cos_ref[z], sin_ref[z]
        q_rot = rotate(qkv_ref[z, 0, 0].astype(jnp.float32), cos_part, sin_part)
        q_s[z] = (q_rot.astype(jnp.bfloat16).astype(jnp.float32) * HD ** (-0.5)).astype(jnp.bfloat16)
        k_rot = rotate(qkv_ref[z, 0, 1].astype(jnp.float32), cos_part, sin_part)
        k_s[at, :] = k_rot.T.astype(jnp.bfloat16)
        v_s[:, at] = qkv_ref[z, 0, 2]

    def block(z, carry):
        scores = mm(k_s[...], q_s[z])
        top = jnp.max(scores, axis=0, keepdims=True)
        exp_scores = jnp.exp(scores - top)
        total = jnp.sum(exp_scores, axis=0, keepdims=True)
        out = mm(v_s[...], exp_scores.astype(jnp.bfloat16))
        out_ref[z, 0] = (out / total).astype(jnp.bfloat16)
        lse_ref[z, 0] = top + jnp.log(total)
        return carry

    lax.fori_loop(0, parts, block, 0)


def attend_back_kernel(
    qkv_ref, cos_ref, sin_ref, out_ref, lse_ref, grad_ref, res_ref,
    q_s, q_rows, k_s, k_cols, v_rows, g_rows, dk, dv,
):
    parts, _, _, _, cols = qkv_ref.shape
    for z in range(parts):
        at = slice(z * cols, (z + 1) * cols)
        cos_part, sin_part = cos_ref[z], sin_ref[z]
        q_rot = rotate(qkv_ref[z, 0, 0].astype(jnp.float32), cos_part, sin_part)
        q_rot = q_rot.astype(jnp.bfloat16).astype(jnp.float32) * HD ** (-0.5)
        q_s[z] = q_rot.astype(jnp.bfloat16)
        q_rows[z] = q_rot.T.astype(jnp.bfloat16)
        k_rot = rotate(qkv_ref[z, 0, 1].astype(jnp.float32), cos_part, sin_part)
        k_cols[:, at] = k_rot.astype(jnp.bfloat16)
        k_s[at, :] = k_rot.T.astype(jnp.bfloat16)
        v_rows[at, :] = qkv_ref[z, 0, 2].astype(jnp.float32).T.astype(jnp.bfloat16)
        g_rows[z] = grad_ref[z, 0].astype(jnp.float32).T.astype(jnp.bfloat16)
    dk[...] = jnp.zeros_like(dk)
    dv[...] = jnp.zeros_like(dv)

    def block(z, carry):
        grad = grad_ref[z, 0]
        inner = jnp.sum(
            grad.astype(jnp.float32) * out_ref[z, 0].astype(jnp.float32), axis=0, keepdims=True
        )
        probs = jnp.exp(mm(k_s[...], q_s[z]) - lse_ref[z, 0])
        dv[...] += mm(probs.astype(jnp.bfloat16), g_rows[z])
        score_grad = (probs * (mm(v_rows[...], grad) - inner)).astype(jnp.bfloat16)
        dk[...] += mm(score_grad, q_rows[z])
        dq = mm(k_cols[...], score_grad) * HD ** (-0.5)
        res_ref[z, 0, 0] = rotate(dq, cos_ref[z], -sin_ref[z]).astype(jnp.bfloat16)
        return carry

    lax.fori_loop(0, parts, block, 0)
    for z in range(parts):
        at = slice(z * cols, (z + 1) * cols)
        dk_cols = dk[at, :].T
        res_ref[z, 0, 1] = rotate(dk_cols, cos_ref[z], -sin_ref[z]).astype(jnp.bfloat16)
        res_ref[z, 0, 2] = dv[at, :].T.astype(jnp.bfloat16)


def pair_spec(parts, *rest):
    zeros = (0,) * len(rest)
    return pl.BlockSpec((parts, 1) + rest, lambda pair: (0, pair) + zeros)


def attend(qkv, cos_tab, sin_tab):
    parts, pairs, _, _, cols = qkv.shape
    length = parts * cols
    table = pl.BlockSpec(cos_tab.shape, lambda pair: (0, 0, 0))
    return pl.pallas_call(
        attend_kernel,
        grid=(pairs,),
        in_specs=[pair_spec(parts, 3, HD, cols), table, table],
        out_specs=[pair_spec(parts, HD, cols), pair_spec(parts, 1, cols)],
        out_shape=[
            jax.ShapeDtypeStruct((parts, pairs, HD, cols), jnp.bfloat16),
            jax.ShapeDtypeStruct((parts, pairs, 1, cols), jnp.float32),
        ],
        scratch_shapes=[
            pltpu.VMEM((parts, HD, cols), jnp.bfloat16),
            pltpu.VMEM((length, HD), jnp.bfloat16),
            pltpu.VMEM((HD, length), jnp.bfloat16),
        ],
        compiler_params=pltpu.CompilerParams(vmem_limit_bytes=40 * 2**20),
        cost_estimate=pl.CostEstimate(
            flops=16 * pairs * length * length * HD,
            bytes_accessed=8 * pairs * length * HD,
            transcendentals=pairs * length * length,
        ),
        name="attend",
    )(qkv, cos_tab, sin_tab)


def attend_back(qkv, cos_tab, sin_tab, out, lse, grad):
    parts, pairs, _, _, cols = qkv.shape
    length = parts * cols
    table = pl.BlockSpec(cos_tab.shape, lambda pair: (0, 0, 0))
    return pl.pallas_call(
        attend_back_kernel,
        grid=(pairs,),
        in_specs=[
            pair_spec(parts, 3, HD, cols),
            table,
            table,
            pair_spec(parts, HD, cols),
            pair_spec(parts, 1, cols),
            pair_spec(parts, HD, cols),
        ],
        out_specs=pair_spec(parts, 3, HD, cols),
        out_shape=jax.ShapeDtypeStruct(qkv.shape, jnp.bfloat16),
        scratch_shapes=[
            pltpu.VMEM((parts, HD, cols), jnp.bfloat16),
            pltpu.VMEM((parts, cols, HD), jnp.bfloat16),
            pltpu.VMEM((length, HD), jnp.bfloat16),
            pltpu.VMEM((HD, length), jnp.bfloat16),
            pltpu.VMEM((length, HD), jnp.bfloat16),
            pltpu.VMEM((parts, cols, HD), jnp.bfloat16),
            pltpu.VMEM((length, HD), jnp.float32),
            pltpu.VMEM((length, HD), jnp.float32),
        ],
        compiler_params=pltpu.CompilerParams(vmem_limit_bytes=48 * 2**20),
        cost_estimate=pl.CostEstimate(
            flops=40 * pairs * length * length * HD,
            bytes_accessed=20 * pairs * length * HD,
            transcendentals=pairs * length * length,
        ),
        name="attend_back",
    )(qkv, cos_tab, sin_tab, out, lse, grad)


def swap(values):
    return lax.ppermute(values, "qblk", [(0, 1), (1, 0)])


def norm_fwd(values, gain_row):
    row_mean = jnp.mean(values, axis=-1, keepdims=True)
    centered = values - row_mean
    row_var = jnp.mean(centered * centered, axis=-1, keepdims=True)
    inv_std = lax.rsqrt(row_var + EPS_NORM)
    normed = centered * inv_std
    return (normed, inv_std, (normed * gain_row).astype(jnp.bfloat16))


def norm_back(upstream, normed, inv_std, gain_row):
    scaled = upstream * gain_row
    return inv_std * (
        scaled
        - jnp.mean(scaled, axis=-1, keepdims=True)
        - normed * jnp.mean(scaled * normed, axis=-1, keepdims=True)
    )


def gated(gate_part, up_part):
    return jax.nn.gelu(gate_part, approximate=False) * up_part


def adam_step(weight, grad_sum, moment, second, learn_rate, weight_decay):
    moment_new = BETA_ONE * moment + (1.0 - BETA_ONE) * grad_sum
    second_new = BETA_TWO * second + (1.0 - BETA_TWO) * grad_sum * grad_sum
    update = (
        moment_new
        / (1.0 - BETA_ONE**STEP)
        / (jnp.sqrt(second_new / (1.0 - BETA_TWO**STEP)) + ADAM_EPS)
    )
    return (moment_new, second_new, weight - learn_rate * (update + weight_decay * weight))


def on_device(
    tokens,
    cotangent,
    w_qkv,
    w_out,
    w_in,
    w_ffn,
    gains,
    first_qkv,
    second_qkv,
    first_out,
    second_out,
    first_in,
    second_in,
    first_ffn,
    second_ffn,
    first_gain,
    second_gain,
):
    n_seq = lax.axis_size("seq")
    core = lax.axis_index("qblk")
    first = core == 0
    seq_count, tok_local, width = tokens.shape
    row_count = seq_count * tok_local
    chip_tok = 2 * tok_local
    heads = H // 2
    pairs = heads * seq_count // n_seq
    both = ("dp", "seq")

    def ordered(own, other, axis):
        return jnp.where(
            first,
            jnp.concatenate([own, other], axis=axis),
            jnp.concatenate([other, own], axis=axis),
        )

    def gather(shard):
        return lax.all_gather(shard, both, axis=0, tiled=True)

    def begin(grad, high_first=False):
        bits = {name: (lax.axis_size(name) - 1).bit_length() for name in both}
        left = [(name, bit) for name in both for bit in reversed(range(bits[name]))]
        steps = sorted(left, key=lambda at: (at[0] != "dp", at[1]))
        if high_first:
            steps = [at for at in left if at[0] == "dp"] + [at for at in steps if at[0] != "dp"]
        rows = grad.shape[0] >> len(left)
        return advance((grad.reshape((2,) * len(left) + (rows, grad.shape[1])), left, steps), 1)

    def advance(state, count):
        held, left, steps = state
        left = list(left)
        for name, bit in steps[:count]:
            dim = left.index((name, bit))
            left.pop(dim)
            own = (lax.axis_index(name) >> bit) & 1
            kept = lax.dynamic_index_in_dim(held, own, dim, keepdims=False)
            sent = lax.dynamic_index_in_dim(held, 1 - own, dim, keepdims=False)
            got = lax.ppermute(
                sent.astype(jnp.bfloat16),
                name,
                [(at, at ^ (1 << bit)) for at in range(lax.axis_size(name))],
            )
            held = kept.astype(jnp.float32) + got.astype(jnp.float32)
            if left:
                held = held.astype(jnp.bfloat16)
        return (held, left, steps[count:])

    def scatter(state):
        return advance(state, len(state[2]))[0]

    def tie(value, states):
        value, helds = lax.optimization_barrier((value, [state[0] for state in states]))
        return value, [(held,) + state[1:] for held, state in zip(helds, states)]

    def with_other(rows):
        return jnp.concatenate([rows, swap(rows)], axis=0)

    def sum_own(part):
        other = swap(part[row_count:].astype(jnp.bfloat16))
        return part[:row_count] + other.astype(jnp.float32)

    third = w_qkv.shape[1] // 3
    low_qkv = w_qkv.astype(jnp.bfloat16)
    col_a, col_b, col_c = low_qkv[:, :third], low_qkv[:, third : 2 * third], low_qkv[:, 2 * third :]
    col_r = swap(col_b)
    low_gain = gains.astype(jnp.bfloat16)
    chip_gain = ordered(low_gain, swap(low_gain), 1).T
    chip_gain = jnp.pad(chip_gain, ((0, 0), (0, 128 - gains.shape[0])))
    shard_qkv = jnp.where(
        first,
        jnp.concatenate([col_a, col_c, col_r], axis=1),
        jnp.concatenate([col_r, col_a, col_c], axis=1),
    )
    full_qkv = gather(jnp.concatenate([shard_qkv, chip_gain], axis=1))
    low_out = w_out.astype(jnp.bfloat16)
    low_in = w_in.astype(jnp.bfloat16)
    part = low_in.shape[1] // 2
    in_r = swap(jnp.where(first, low_in[:, part:], low_in[:, :part]))
    shard_gate = jnp.where(first, low_in[:, :part], in_r)
    shard_up = jnp.where(first, in_r, low_in[:, part:])
    low_ffn = w_ffn.astype(jnp.bfloat16)
    full_qkv, low_out, shard_gate, shard_up, low_ffn = lax.optimization_barrier(
        (full_qkv, low_out, shard_gate, shard_up, low_ffn)
    )
    full_gain = full_qkv[:, 3 * third : 3 * third + gains.shape[0]].T
    full_qkv = full_qkv[:, : 3 * third]
    half_out = gather(low_out)
    full_out = ordered(half_out, swap(half_out), 1)
    full_gate = gather(shard_gate)
    full_up = gather(shard_up)
    full_ffn = gather(low_ffn)

    place_ids = jnp.arange(n_seq * chip_tok, dtype=jnp.int32).reshape(n_seq, 1, chip_tok)
    in_chip = place_ids % chip_tok
    positions = (
        place_ids - in_chip + (in_chip // tok_local + core) % 2 * tok_local + in_chip % tok_local
    ).astype(jnp.float32)
    half_dim = HD // 2
    inv_freq = ROPE_BASE ** (-2.0 * jnp.arange(half_dim, dtype=jnp.float32) / HD)
    angles = inv_freq[None, :, None] * positions
    cos_tab, sin_tab = jnp.cos(angles), jnp.sin(angles)

    def to_heads(cols, kinds):
        split = cols.reshape(kinds, heads, HD, 2, seq_count, tok_local)
        split = split.transpose(1, 4, 0, 2, 3, 5).reshape(n_seq, pairs, kinds, HD, chip_tok)
        return lax.all_to_all(split, "seq", split_axis=0, concat_axis=0, tiled=True)

    def from_heads(moved, kinds):
        back = lax.all_to_all(moved, "seq", split_axis=0, concat_axis=0, tiled=True)
        back = back.reshape(heads, seq_count, kinds, HD, 2, tok_local)
        return back.transpose(2, 0, 3, 4, 1, 5).reshape(kinds * heads * HD, 2 * row_count)

    gain_rows = full_gain.astype(jnp.float32)
    resid_in = tokens.astype(jnp.float32).reshape(row_count, width)
    normed_one, inv_one, attn_own = norm_fwd(resid_in, gain_rows[0])
    attn_in = with_other(attn_own)
    grad_own = cotangent.reshape(row_count, width).astype(jnp.bfloat16)
    grad_low = with_other(grad_own)
    proj = jnp.einsum("dn,td->nt", full_qkv, attn_in, preferred_element_type=jnp.float32)
    qkv = to_heads(proj.astype(jnp.bfloat16), 3)
    head_out, lse = attend(qkv, cos_tab, sin_tab)
    attn_cols = from_heads(head_out[:, :, None], 1)
    attn = ordered(attn_cols[:, :row_count], swap(attn_cols[:, row_count:]), 0)
    resid_mid = resid_in + jnp.einsum(
        "ft,fd->td", attn, full_out, preferred_element_type=jnp.float32
    )
    normed_two, inv_two, ffn_own = norm_fwd(resid_mid, gain_rows[1])
    ffn_in = with_other(ffn_own)
    gate_part = mm(ffn_in, full_gate)
    up_part = mm(ffn_in, full_up)
    hidden = gated(gate_part, up_part).astype(jnp.bfloat16)
    hidden_grad = mm(grad_low, full_ffn)
    gate_grad, up_grad = jax.vjp(gated, gate_part, up_part)[1](hidden_grad)
    gate_grad = gate_grad.astype(jnp.bfloat16)
    up_grad = up_grad.astype(jnp.bfloat16)

    def outer(left, right):
        return jnp.einsum("ta,tb->ab", left, right, preferred_element_type=jnp.float32).astype(
            jnp.bfloat16
        )

    def times_t(left, right):
        return jnp.einsum("tf,df->td", left, right, preferred_element_type=jnp.float32)

    ffn_in_grad = sum_own(times_t(gate_grad, full_gate) + times_t(up_grad, full_up))
    gain_two_grad = jnp.sum(ffn_in_grad * normed_two, axis=0)
    grad_y = cotangent.astype(jnp.float32).reshape(row_count, width)
    mid_grad = grad_y + norm_back(ffn_in_grad, normed_two, inv_two, gain_rows[1])
    mid_low = mid_grad.astype(jnp.bfloat16)
    grad_gate = outer(ffn_in, gate_grad)
    grad_up = outer(ffn_in, up_grad)
    grad_ffn = outer(grad_low, hidden)
    attn_grad = jnp.einsum("fd,td->ft", full_out, mid_low, preferred_element_type=jnp.float32)
    attn_grad = attn_grad.astype(jnp.bfloat16)
    span = heads * HD
    mine = lax.dynamic_slice_in_dim(attn_grad, core * span, span, axis=0)
    theirs = lax.dynamic_slice_in_dim(attn_grad, (1 - core) * span, span, axis=0)
    heads_grad = to_heads(jnp.concatenate([mine, swap(theirs)], axis=1), 1)
    heads_grad, grad_gate, grad_up, grad_ffn = lax.optimization_barrier(
        (heads_grad, grad_gate, grad_up, grad_ffn)
    )
    states = [begin(grad_gate), begin(grad_up, True), begin(grad_ffn)]
    grad_out = jnp.einsum("ft,td->fd", attn, mid_low, preferred_element_type=jnp.float32)
    out_cols = w_out.shape[1]
    out_mine = lax.dynamic_slice_in_dim(grad_out, core * out_cols, out_cols, axis=1)
    out_theirs = lax.dynamic_slice_in_dim(grad_out, (1 - core) * out_cols, out_cols, axis=1)
    out_sum = out_mine + swap(out_theirs.astype(jnp.bfloat16)).astype(jnp.float32)
    states.append(begin(out_sum.astype(jnp.bfloat16), True))
    block_part = times_t(hidden, full_ffn)
    block_out = (resid_mid + sum_own(block_part)).astype(jnp.bfloat16).reshape(tokens.shape)

    res = attend_back(qkv, cos_tab, sin_tab, head_out, lse, heads_grad[:, :, 0])
    res, states = tie(res, states)
    states = [advance(state, 1) for state in states]
    qkv_grad = from_heads(res, 3)
    qkv_grad, states = tie(qkv_grad, states)
    sum_gate, sum_up, sum_ffn, sum_out = [scatter(state) for state in states]
    grad_qkv = jnp.einsum("td,nt->dn", attn_in, qkv_grad, preferred_element_type=jnp.float32)
    in_grad = sum_own(
        jnp.einsum("nt,dn->td", qkv_grad, full_qkv, preferred_element_type=jnp.float32)
    )
    gain_one_grad = jnp.sum(in_grad * normed_one, axis=0)
    grad_x = mid_grad + norm_back(in_grad, normed_one, inv_one, gain_rows[0])
    gain_cols = jnp.stack([gain_one_grad, gain_two_grad], axis=1)
    gain_cols = jnp.pad(gain_cols, ((0, 0), (0, 128 - gain_cols.shape[1])))
    low_rows = jnp.concatenate([grad_qkv, gain_cols], axis=1).astype(jnp.bfloat16)
    rows_qkv = scatter(begin(low_rows))
    gain_rows_sum = rows_qkv[:, 3 * third : 3 * third + gains.shape[0]].T
    rows_qkv = rows_qkv[:, : 3 * third]
    gain_wide = gains.shape[1]
    gain_mine = lax.dynamic_slice_in_dim(gain_rows_sum, core * gain_wide, gain_wide, axis=1)
    gain_theirs = lax.dynamic_slice_in_dim(gain_rows_sum, (1 - core) * gain_wide, gain_wide, axis=1)
    sum_gain = gain_mine + swap(gain_theirs.astype(jnp.bfloat16)).astype(jnp.float32)
    q_sum, k_sum, v_sum = rows_qkv[:, :third], rows_qkv[:, third : 2 * third], rows_qkv[:, 2 * third :]
    qkv_r = swap(jnp.where(first, v_sum, q_sum).astype(jnp.bfloat16)).astype(jnp.float32)
    sum_qkv = jnp.concatenate(
        [jnp.where(first, q_sum, k_sum), qkv_r, jnp.where(first, k_sum, v_sum)], axis=1
    )
    gate_up_r = swap(jnp.where(first, sum_up, sum_gate).astype(jnp.bfloat16)).astype(jnp.float32)
    sum_in = ordered(jnp.where(first, sum_gate, sum_up), gate_up_r, 1)
    new_qkv = adam_step(
        w_qkv, sum_qkv, first_qkv, second_qkv, LR_FACTOR * D ** (-0.5), WEIGHT_DECAY
    )
    new_out = adam_step(
        w_out, sum_out, first_out, second_out, LR_FACTOR * OUT_FAN ** (-0.5), WEIGHT_DECAY
    )
    new_in = adam_step(w_in, sum_in, first_in, second_in, LR_FACTOR * D ** (-0.5), WEIGHT_DECAY)
    new_ffn = adam_step(
        w_ffn, sum_ffn, first_ffn, second_ffn, LR_FACTOR * FF ** (-0.5), WEIGHT_DECAY
    )
    new_gain = adam_step(gains, sum_gain, first_gain, second_gain, LR_GAIN, 0.0)
    return (
        block_out,
        grad_x.reshape(tokens.shape),
        new_qkv[0],
        new_qkv[1],
        new_qkv[2],
        new_out[0],
        new_out[1],
        new_out[2],
        new_in[0],
        new_in[1],
        new_in[2],
        new_ffn[0],
        new_ffn[1],
        new_ffn[2],
        new_gain[0],
        new_gain[1],
        new_gain[2],
    )


def solution(mesh):
    placed = (
        P("dp", ("seq", "qblk"), None),
        P("dp", ("seq", "qblk"), None),
        P(("dp", "seq"), "qblk"),
        P(("dp", "seq"), "qblk"),
        P(("dp", "seq"), "qblk"),
        P(("dp", "seq"), "qblk"),
        P(None, ("dp", "seq", "qblk")),
        P(("dp", "seq"), "qblk"),
        P(("dp", "seq"), "qblk"),
        P(("dp", "seq"), "qblk"),
        P(("dp", "seq"), "qblk"),
        P(("dp", "seq"), "qblk"),
        P(("dp", "seq"), "qblk"),
        P(("dp", "seq"), "qblk"),
        P(("dp", "seq"), "qblk"),
        P(None, ("dp", "seq", "qblk")),
        P(None, ("dp", "seq", "qblk")),
    )
    return jax.shard_map(
        on_device,
        mesh=mesh,
        in_specs=placed,
        out_specs=(
            P("dp", ("seq", "qblk"), None),
            P("dp", ("seq", "qblk"), None),
            P(("dp", "seq"), "qblk"),
            P(("dp", "seq"), "qblk"),
            P(("dp", "seq"), "qblk"),
            P(("dp", "seq"), "qblk"),
            P(("dp", "seq"), "qblk"),
            P(("dp", "seq"), "qblk"),
            P(("dp", "seq"), "qblk"),
            P(("dp", "seq"), "qblk"),
            P(("dp", "seq"), "qblk"),
            P(("dp", "seq"), "qblk"),
            P(("dp", "seq"), "qblk"),
            P(("dp", "seq"), "qblk"),
            P(None, ("dp", "seq", "qblk")),
            P(None, ("dp", "seq", "qblk")),
            P(None, ("dp", "seq", "qblk")),
        ),
        check_vma=False,
    )
```
